256 devices in a mesh: dp: 16 (over z_hi, x, core), mp: 16 (over z_lo, y).
Axes of the slice: x: 4, y: 4, z: 8 (z_hi: 2, z_lo: 4; z = z_hi * 4 + z_lo), core: 2. Of those that a mesh axis runs over, the one named last changes fastest.
Arguments:
- acts: bfloat16 [2048, 8192], P('dp', 'mp'), may hold values from -6 to 6
- grad_out: bfloat16 [2048, 14336], P('dp', 'mp'), may hold values from -6 to 6
- values: bfloat16 [112, 20, 128, 128], P('mp', None, 'dp'), may hold values from -0.125 to 0.125
- block_rows: int32 [112, 20], P('mp'), may hold values from 0 to 63, as said below
- block_count: int32 [112], P('mp'), may hold values from 12 to 20, as said below
Outputs:
- hidden_out: bfloat16 [2048, 14336], P('dp', 'mp')
- grad_acts: bfloat16 [2048, 8192], P('dp', 'mp')
- grad_values: float32 [112, 20, 128, 128], P('mp', None, 'dp')
The draws below stay inside these ranges and needn't reach their ends.
Inputs may be any that keep to these rules, and one draw needn't show every extreme that they name: `block_rows`: the live slots of a block column name distinct block rows; the first ones follow a butterfly pattern around block row c % 64. Slots at or after block_count are ignored. `block_count`: some block column has all 20 slots live.
All inputs are finite; a program needn't handle non-finite values.
Results may differ from the reference program's by a relative error of at most 0.02.
Values may be sent and summed in bfloat16 or wider, within the bound.
No kernel may reach another device: no remote copies, remote signals or barrier semaphores. Data moves between devices by JAX's collectives and lax.ppermute only.
A program may use at most 128 MiB of HBM per device.

```python
import jax
import jax.numpy as jnp
from jax import lax

D = 8192
BLK = 128
CB_DEV = 7
KMAX = 20
KMIN = 12
NCB = 112
FF = 14336
TOKENS = 2048
N_MP = 16


def draw_block_rows(key, part):
    key = jax.random.fold_in(key, 11)
    row_blocks = D // BLK
    columns = jnp.arange(NCB, dtype=jnp.int32)[:, None]
    positions = jnp.arange(row_blocks, dtype=jnp.int32)[None, :]
    flipped = jnp.bitwise_xor(columns % row_blocks, positions)
    butterfly = jnp.bitwise_and(flipped, flipped - 1) == 0
    noise = jax.random.randint(key, (NCB, row_blocks), 0, 2 ** 20, dtype=jnp.int32)
    scores = jnp.where(butterfly, 2 ** 27, 0) + noise * row_blocks + positions
    order = jnp.argsort(-scores, axis=1, stable=True)
    return order[:, :KMAX].astype(jnp.int32)


def draw_block_count(key, part):
    key = jax.random.fold_in(key, 23)
    first, second = jax.random.split(key)
    counts = jax.random.randint(first, (NCB,), KMIN, KMAX + 1, dtype=jnp.int32)
    fullest = jax.random.randint(second, (), 0, NCB, dtype=jnp.int32)
    return counts.at[fullest].set(KMAX).astype(jnp.int32)


def steps_of(own_key, dims, cuts, smallest, top_value):
    def one(axis_at, shards_of):
        heights = jax.random.uniform(jax.random.fold_in(jax.random.fold_in(own_key, 6), axis_at), (shards_of,), jnp.float32, smallest / len(cuts), top_value / len(cuts))
        return jnp.repeat(jnp.exp(heights), dims[axis_at] // shards_of).reshape((-1,) + (1,) * (len(dims) - axis_at - 1))

    factor_of = one(*cuts[0])
    for cut in cuts[1:]:
        factor_of = factor_of * one(*cut)
    return factor_of


def scatter_about(stream_key, dims, width, most, shards=(), kind=jnp.bfloat16):
    values = jax.random.normal(stream_key, dims, jnp.float32) * width
    if len(shards) > 0:
        values = steps_of(stream_key, dims, shards, -0.22, 0.18) * values
    return jnp.clip(values, min=-most, max=most).astype(kind)


def setup_inputs(seed: int = 0) -> dict:
    streams_of = jax.random.split(jax.random.key(seed), 6)
    return {
        "acts": scatter_about(streams_of[0], (TOKENS, D), 1.0, 6.0, ((0, 16), (1, 16))),
        "grad_out": scatter_about(streams_of[1], (TOKENS, FF), 1.0, 6.0, ((0, 16), (1, 16))),
        "values": scatter_about(streams_of[2], (NCB, KMAX, BLK, BLK), (KMAX * BLK) ** -0.5, 0.125, ((0, 16), (2, 16))),
        "block_rows": draw_block_rows(jax.random.fold_in(streams_of[5], 71), 0),
        "block_count": draw_block_count(jax.random.fold_in(streams_of[5], 71), 0),
    }


def reference(acts, grad_out, values, block_rows, block_count):
    row_blocks = D // BLK
    blocked = acts.reshape(TOKENS, row_blocks, BLK).astype(jnp.float32)
    grad_blocks = grad_out.reshape(TOKENS, NCB, BLK).astype(jnp.float32)
    slot_live = jnp.arange(KMAX, dtype=jnp.int32)[None, :] < block_count[:, None]
    masked = jnp.where(slot_live[:, :, None, None], values.astype(jnp.float32), jnp.zeros((), jnp.float32))

    def per_column(column):
        rows = block_rows[column]
        picked = jnp.take(blocked, rows, axis=1)
        upstream = grad_blocks[:, column]
        produced = jnp.einsum("tki,kij->tj", picked, masked[column])
        weight_grad = jnp.einsum("tki,tj->kij", picked, upstream)
        weight_grad = jnp.where(slot_live[column][:, None, None], weight_grad, jnp.zeros((), jnp.float32))
        return produced, weight_grad

    produced, grad_values = lax.map(per_column, jnp.arange(NCB, dtype=jnp.int32))
    hidden_out = jnp.transpose(produced, (1, 0, 2)).reshape(TOKENS, NCB * BLK).astype(jnp.bfloat16)

    def per_group(total, group):
        def add_column(offset, partial_value):
            column = group * CB_DEV + offset
            rows = block_rows[column]
            contrib = jnp.einsum("tj,kij->tki", grad_blocks[:, column], masked[column])
            return partial_value.at[:, rows].add(contrib)

        partial_value = lax.fori_loop(0, CB_DEV, add_column, jnp.zeros((TOKENS, row_blocks, BLK), jnp.float32))
        rounded = lax.optimization_barrier(partial_value.astype(jnp.bfloat16)).astype(jnp.float32)
        return total + rounded, None

    total, unused = lax.scan(per_group, jnp.zeros((TOKENS, row_blocks, BLK), jnp.float32), jnp.arange(N_MP, dtype=jnp.int32))
    grad_acts = total.reshape(TOKENS, D).astype(jnp.bfloat16)
    return hidden_out, grad_acts, grad_values
```

```python
import functools

import jax
import jax.numpy as jnp
from jax import lax
from jax.experimental import pallas as pl
from jax.experimental.pallas import tpu as pltpu
from jax.sharding import PartitionSpec as P

NZ = 4
NY = 4
NX = 4
BLK = 128
VMEM_LIMIT = 40 * 1024 * 1024


def y_pairs(shift):
    return [(z * NY + y, z * NY + (y + shift) % NY) for z in range(NZ) for y in range(NY)]


def z_pairs(shift):
    return [(z * NY + y, (z + shift) % NZ * NY + y) for z in range(NZ) for y in range(NY)]


def x_pairs(shift):
    return [
        ((h * NX + x) * 2 + c, (h * NX + (x + shift) % NX) * 2 + c)
        for h in range(2)
        for x in range(NX)
        for c in range(2)
    ]


CORE_PAIRS = [(i, i ^ 1) for i in range(16)]
HALF_PAIRS = [(i, i ^ 8) for i in range(16)]


def block_grads(cols, half, pos_ref, chip_ref, acts_ref, up_ref, *outs):
    def column(c, carry):
        up = up_ref[:, pl.ds(pl.multiple_of(c * BLK, BLK), BLK)]
        for h, out in enumerate(outs):
            for k in range(half):
                slot = c * half + k
                block = acts_ref[pos_ref[h * cols * half + slot]]
                grad = lax.dot_general(
                    block, up, (((0,), (0,)), ((), ())), preferred_element_type=jnp.float32
                ).astype(jnp.bfloat16)
                for chip in range(8):
                    out[chip_ref[chip], slot] = grad[chip * 16 : (chip + 1) * 16]
        return carry

    lax.fori_loop(0, cols, column, 0)


def project(cols, half, pos_ref, chip_ref, acts_ref, up_ref, w0_ref, w1_ref, hidden_ref, *rest):
    parts, total = rest[:-1], rest[-1]
    total[...] = jnp.zeros_like(total)

    def column(c, carry):
        lanes = pl.ds(pl.multiple_of(c * BLK, BLK), BLK)
        up = up_ref[:, lanes]
        hidden = jnp.zeros((up.shape[0], BLK), jnp.float32)
        for h, w_ref in enumerate((w0_ref, w1_ref)):
            for k in range(0, half, 2):
                rows = []
                blocks = []
                weights = []
                for j in range(2):
                    slot = c * half + k + j
                    rows.append(pos_ref[h * cols * half + slot])
                    blocks.append(acts_ref[rows[-1]])
                    weights += [w_ref[chip_ref[chip], slot] for chip in range(8)]
                weight = jnp.concatenate(weights, axis=0)
                hidden += jnp.dot(
                    jnp.concatenate(blocks, axis=1), weight, preferred_element_type=jnp.float32
                )
                back = lax.dot_general(
                    up, weight, (((1,), (1,)), ((), ())), preferred_element_type=jnp.float32
                )
                for j in range(2):
                    total[rows[j]] += back[:, j * BLK : (j + 1) * BLK]
        hidden_ref[:, lanes] = hidden.astype(jnp.bfloat16)
        return carry

    lax.fori_loop(0, cols, column, 0)
    step = total.shape[0] // len(parts)
    for p, part in enumerate(parts):
        part[...] = total[p * step : (p + 1) * step].astype(jnp.bfloat16)


def kernel_call(body, outs, scratch, flops, ins):
    specs = [pl.BlockSpec(memory_space=pltpu.SMEM)] * 2
    specs += [pl.BlockSpec(memory_space=pltpu.VMEM)] * (len(ins) - 2)
    moved = sum(a.size * a.dtype.itemsize for a in list(ins) + list(outs))
    return pl.pallas_call(
        body,
        out_shape=outs,
        in_specs=specs,
        out_specs=[pl.BlockSpec(memory_space=pltpu.VMEM)] * len(outs),
        scratch_shapes=scratch,
        compiler_params=pltpu.CompilerParams(vmem_limit_bytes=VMEM_LIMIT),
        cost_estimate=pl.CostEstimate(flops=flops, bytes_accessed=moved, transcendentals=0),
    )(*ins)


def f32(a):
    return a.astype(jnp.float32)


def shards(acts, grad_out, values, block_rows, block_count):
    tokens = acts.shape[0]
    cols, slots = block_rows.shape
    half = slots // 2
    own_blocks = acts.shape[1] // BLK
    bf = jnp.bfloat16
    dp, mp = lax.axis_index("dp"), lax.axis_index("mp")
    core, x, zh = dp % 2, dp // 2 % NX, dp // (2 * NX)
    z, y = mp // NY, mp % NY
    first = core == 0

    def halves(a):
        return (
            jnp.where(first, a[:, :half], a[:, half:]),
            jnp.where(first, a[:, half:], a[:, :half]),
        )

    def ordered(mine, other, axis):
        return jnp.where(
            first,
            jnp.concatenate([mine, other], axis=axis),
            jnp.concatenate([other, mine], axis=axis),
        )

    live = jnp.arange(slots, dtype=jnp.int32)[None, :] < block_count[:, None]
    block = jnp.clip(block_rows, 0, NZ * NY * own_blocks - 1)
    owner = block // own_blocks
    place = ((y - owner % NY) % NY * NZ + (z - owner // NY) % NZ) * own_blocks + block % own_blocks
    pos = jnp.concatenate([a.reshape(-1) for a in halves(place)])
    chips = jnp.arange(8, dtype=jnp.int32)
    chip = (x - chips % NX) % NX * 2 + (zh + chips // NX) % 2

    masked = jnp.where(live[:, :, None, None], values, jnp.zeros((), bf))
    mine, other = halves(masked)
    came = lax.ppermute(other, "dp", CORE_PAIRS)
    rows16 = ordered(mine, came, 2).reshape(cols * half, 16, BLK)

    own = acts.reshape(tokens, own_blocks, BLK).transpose(1, 0, 2)
    along_z = jnp.concatenate([own] + [lax.ppermute(own, "mp", z_pairs(q)) for q in range(1, NZ)])

    w2 = jnp.stack([rows16, lax.ppermute(rows16, "dp", HALF_PAIRS)])
    whole = jnp.concatenate(
        [along_z] + [lax.ppermute(along_z, "mp", y_pairs(p)) for p in range(1, NY)]
    )
    w8 = jnp.concatenate([w2] + [lax.ppermute(w2, "dp", x_pairs(s)) for s in range(1, NX)])
    w8_other = lax.ppermute(w8, "dp", CORE_PAIRS)

    flops = 2 * tokens * BLK * BLK * cols * slots
    shape = jax.ShapeDtypeStruct((8, cols * half, 16, BLK), bf)
    mine, other = kernel_call(
        functools.partial(block_grads, cols, half),
        [shape, shape],
        [],
        flops,
        (pos, chip, whole, grad_out),
    )
    came = lax.ppermute(other, "dp", CORE_PAIRS)
    sums = [(f32(mine[s * 2 : s * 2 + 2]) + f32(came[s * 2 : s * 2 + 2])).astype(bf) for s in range(NX)]
    came = [lax.ppermute(sums[s], "dp", x_pairs(-s)) for s in range(1, NX)]
    total = f32(sums[0]) + f32(came[0]) + f32(came[1]) + f32(came[2])
    came = lax.ppermute(total[1].astype(bf), "dp", HALF_PAIRS)
    total = (total[0] + f32(came)).reshape(cols, half, 16, BLK)
    keep = jnp.where(first, total[:, :, :8], total[:, :, 8:])
    send = jnp.where(first, total[:, :, 8:], total[:, :, :8])
    grad_values = ordered(keep, lax.ppermute(send, "dp", CORE_PAIRS), 1)
    grad_values = jnp.where(live[:, :, None, None], grad_values, jnp.zeros((), jnp.float32))

    part = jax.ShapeDtypeStruct((NZ * own_blocks, tokens, BLK), bf)
    hidden_out, *parts = kernel_call(
        functools.partial(project, cols, half),
        [jax.ShapeDtypeStruct(grad_out.shape, bf)] + [part] * NY,
        [pltpu.VMEM((NZ * NY * own_blocks, tokens, BLK), jnp.float32)],
        2 * flops,
        (pos, chip, whole, grad_out, w8, w8_other),
    )
    came = [lax.ppermute(parts[p], "mp", y_pairs(-p)) for p in range(1, NY)]

    def summed(q):
        at = slice(q * own_blocks, (q + 1) * own_blocks)
        return f32(parts[0][at]) + f32(came[0][at]) + f32(came[1][at]) + f32(came[2][at])

    total = summed(0)
    for q in range(1, NZ):
        total += f32(lax.ppermute(summed(q).astype(bf), "mp", z_pairs(-q)))
    grad_acts = total.transpose(1, 0, 2).reshape(tokens, own_blocks * BLK).astype(bf)
    return hidden_out, grad_acts, grad_values


def solution(mesh):
    placed = (P("dp", "mp"), P("dp", "mp"), P("mp", None, "dp", None), P("mp", None), P("mp"))
    return jax.shard_map(
        shards,
        mesh=mesh,
        in_specs=placed,
        out_specs=(P("dp", "mp"), P("dp", "mp"), P("mp", None, "dp", None)),
        check_vma=False,
    )
```

```python
import functools

import jax
import jax.numpy as jnp
from jax import lax
from jax.experimental import pallas as pl
from jax.experimental.pallas import tpu as pltpu
from jax.sharding import PartitionSpec as P

NZ = 4
NY = 4
NX = 4
BLK = 128
VMEM_LIMIT = 40 * 1024 * 1024


def y_pairs(shift):
    return [(z * NY + y, z * NY + (y + shift) % NY) for z in range(NZ) for y in range(NY)]


def z_pairs(shift):
    return [(z * NY + y, (z + shift) % NZ * NY + y) for z in range(NZ) for y in range(NY)]


def x_pairs(shift):
    return [
        ((h * NX + x) * 2 + c, (h * NX + (x + shift) % NX) * 2 + c)
        for h in range(2)
        for x in range(NX)
        for c in range(2)
    ]


CORE_PAIRS = [(i, i ^ 1) for i in range(16)]
HALF_PAIRS = [(i, i ^ 8) for i in range(16)]


def block_grads(cols, half, pos_ref, chip_ref, acts_ref, up_ref, *outs):
    def column(c, carry):
        up = up_ref[:, pl.ds(pl.multiple_of(c * BLK, BLK), BLK)]
        for h, out in enumerate(outs):
            for k in range(half):
                slot = c * half + k
                block = acts_ref[pos_ref[h * cols * half + slot]]
                grad = lax.dot_general(
                    block, up, (((0,), (0,)), ((), ())), preferred_element_type=jnp.float32
                ).astype(jnp.bfloat16)
                for chip in range(8):
                    out[chip_ref[chip], slot] = grad[chip * 16 : (chip + 1) * 16]
        return carry

    lax.fori_loop(0, cols, column, 0)


def project(cols, half, pos_ref, chip_ref, acts_ref, up_ref, w0_ref, w1_ref, hidden_ref, *rest):
    parts, total = rest[:-1], rest[-1]
    total[...] = jnp.zeros_like(total)

    def column(c, carry):
        lanes = pl.ds(pl.multiple_of(c * BLK, BLK), BLK)
        up = up_ref[:, lanes]
        hidden = jnp.zeros((up.shape[0], BLK), jnp.float32)
        for h, w_ref in enumerate((w0_ref, w1_ref)):
            for k in range(0, half, 2):
                rows = []
                blocks = []
                weights = []
                for j in range(2):
                    slot = c * half + k + j
                    rows.append(pos_ref[h * cols * half + slot])
                    blocks.append(acts_ref[rows[-1]])
                    weights += [w_ref[chip_ref[chip], slot] for chip in range(8)]
                weight = jnp.concatenate(weights, axis=0)
                hidden += jnp.dot(
                    jnp.concatenate(blocks, axis=1), weight, preferred_element_type=jnp.float32
                )
                back = lax.dot_general(
                    up, weight, (((1,), (1,)), ((), ())), preferred_element_type=jnp.float32
                )
                for j in range(2):
                    total[rows[j]] += back[:, j * BLK : (j + 1) * BLK]
        hidden_ref[:, lanes] = hidden.astype(jnp.bfloat16)
        return carry

    lax.fori_loop(0, cols, column, 0)
    start = 0
    for part in parts:
        part[...] = total[start : start + part.shape[0]].astype(jnp.bfloat16)
        start += part.shape[0]


def kernel_call(body, outs, scratch, flops, ins):
    specs = [pl.BlockSpec(memory_space=pltpu.SMEM)] * 2
    specs += [pl.BlockSpec(memory_space=pltpu.VMEM)] * (len(ins) - 2)
    moved = sum(a.size * a.dtype.itemsize for a in list(ins) + list(outs))
    return pl.pallas_call(
        body,
        out_shape=outs,
        in_specs=specs,
        out_specs=[pl.BlockSpec(memory_space=pltpu.VMEM)] * len(outs),
        scratch_shapes=scratch,
        compiler_params=pltpu.CompilerParams(vmem_limit_bytes=VMEM_LIMIT),
        cost_estimate=pl.CostEstimate(flops=flops, bytes_accessed=moved, transcendentals=0),
    )(*ins)


def f32(a):
    return a.astype(jnp.float32)


def z_step(a, q):
    with jax.named_scope("z_lo"):
        return lax.ppermute(a, "mp", z_pairs(q))


def y_step(a, p):
    with jax.named_scope("y"):
        return lax.ppermute(a, "mp", y_pairs(p))


def x_step(a, s):
    with jax.named_scope("x"):
        return lax.ppermute(a, "dp", x_pairs(s))


def zh_step(a):
    with jax.named_scope("z_hi"):
        return lax.ppermute(a, "dp", HALF_PAIRS)


def core_step(a):
    with jax.named_scope("core"):
        return lax.ppermute(a, "dp", CORE_PAIRS)


def tie(values, *after):
    return lax.optimization_barrier((values, after))[0]


def gather_direct(step, a):
    return [a] + [step(a, s) for s in range(1, 4)]


def gather_passed(step, a):
    n = a.shape[0] // 2
    back, ahead = step(a, 1), step(a, -1)
    opposite = jnp.concatenate([step(back[:n], 1), step(ahead[n:], -1)])
    return [a, back, opposite, ahead]


def sum_direct(step, p0, p1, p2a, p2b, p3):
    return f32(p0) + f32(step(p1, -1)) + f32(step(jnp.concatenate([p2a, p2b]), -2)) + f32(step(p3, -3))


def sum_passed(step, p0, p1, p2a, p2b, p3):
    n = p2a.shape[0]
    ahead, back = step(p2a, 1), step(p2b, -1)
    p3 = jnp.concatenate([(f32(p3[:n]) + f32(ahead)).astype(p3.dtype), p3[n:]])
    p1 = jnp.concatenate([p1[:n], (f32(p1[n:]) + f32(back)).astype(p1.dtype)])
    return f32(p0) + f32(step(p3, 1)) + f32(step(p1, -1))


def shards(acts, grad_out, values, block_rows, block_count):
    tokens = acts.shape[0]
    cols, slots = block_rows.shape
    half = slots // 2
    own_blocks = acts.shape[1] // BLK
    bf = jnp.bfloat16
    dp, mp = lax.axis_index("dp"), lax.axis_index("mp")
    core, x, zh = dp % 2, dp // 2 % NX, dp // (2 * NX)
    z, y = mp // NY, mp % NY
    first = core == 0

    def halves(a):
        return (
            jnp.where(first, a[:, :half], a[:, half:]),
            jnp.where(first, a[:, half:], a[:, :half]),
        )

    def ordered(mine, other, axis):
        return jnp.where(
            first,
            jnp.concatenate([mine, other], axis=axis),
            jnp.concatenate([other, mine], axis=axis),
        )

    blocks = NZ * NY * own_blocks
    live = jnp.arange(slots, dtype=jnp.int32)[None, :] < block_count[:, None]
    owner = block_rows // own_blocks
    place = ((y - owner % NY) % NY * NZ + (z - owner // NY) % NZ) * own_blocks + block_rows % own_blocks
    place = jnp.where(live, place, blocks)
    pos = jnp.concatenate([a.reshape(-1) for a in halves(place)])
    chips = jnp.arange(8, dtype=jnp.int32)
    chip = (zh + chips // NX) % 2 * NX + (x - chips % NX) % NX

    mine, other = halves(values)
    rows16 = ordered(mine, core_step(other), 2).reshape(cols * half, 16, BLK)

    own = acts.reshape(tokens, own_blocks, BLK).transpose(1, 0, 2)
    along_z = jnp.concatenate([own] + [z_step(own, q) for q in range(1, NZ)])
    far16 = zh_step(rows16)
    near = gather_direct(x_step, rows16)
    along_z = tie(along_z, rows16)
    whole = gather_passed(y_step, along_z)
    far = gather_direct(x_step, far16)
    whole = jnp.concatenate(whole + [jnp.zeros((1, tokens, BLK), bf)])
    w8 = jnp.stack(near + far)
    w8_other = core_step(w8)

    flops = 2 * tokens * BLK * BLK * cols * slots
    shape = jax.ShapeDtypeStruct((8, cols * half, 16, BLK), bf)
    mine, other = kernel_call(
        functools.partial(block_grads, cols, half),
        [shape, shape],
        [],
        flops,
        (pos, chip, whole, grad_out),
    )
    came = core_step(other)

    part = jax.ShapeDtypeStruct((NZ * own_blocks, tokens, BLK), bf)
    half_part = jax.ShapeDtypeStruct((NZ * own_blocks // 2, tokens, BLK), bf)
    hidden_out, *parts = kernel_call(
        functools.partial(project, cols, half),
        [jax.ShapeDtypeStruct(grad_out.shape, bf), part, part, half_part, half_part, part],
        [pltpu.VMEM((blocks + 1, tokens, BLK), jnp.float32)],
        2 * flops,
        (pos, chip, whole, grad_out, w8, w8_other),
    )

    def over_x(zr, after=None):
        sums = [(f32(mine[zr * NX + s]) + f32(came[zr * NX + s])).astype(bf) for s in range(NX)]
        if after is not None:
            sums = tie(sums, after)
        n = sums[2].shape[0] // 2
        return sum_passed(x_step, sums[0], sums[1], sums[2][:n], sums[2][n:], sums[3])

    away = over_x(1).astype(bf)
    total = over_x(0, away)
    away = zh_step(away)
    total = (total + f32(away)).reshape(cols, half, 16, BLK)
    keep = jnp.where(first, total[:, :, :8], total[:, :, 8:])
    send = jnp.where(first, total[:, :, 8:], total[:, :, :8])
    grad_values = ordered(keep, core_step(send), 1)

    rest = sum_passed(y_step, *parts)
    total = rest[:own_blocks]
    for q in range(1, NZ):
        total += f32(z_step(rest[q * own_blocks : (q + 1) * own_blocks].astype(bf), -q))
    grad_acts = total.transpose(1, 0, 2).reshape(tokens, own_blocks * BLK).astype(bf)
    return hidden_out, grad_acts, grad_values


def solution(mesh):
    placed = (P("dp", "mp"), P("dp", "mp"), P("mp", None, "dp", None), P("mp", None), P("mp"))
    return jax.shard_map(
        shards,
        mesh=mesh,
        in_specs=placed,
        out_specs=(P("dp", "mp"), P("dp", "mp"), P("mp", None, "dp", None)),
        check_vma=False,
    )
```

```python
import functools

import jax
import jax.numpy as jnp
from jax import lax
from jax.experimental import pallas as pl
from jax.experimental.pallas import tpu as pltpu
from jax.sharding import PartitionSpec as P

NZ = 4
NY = 4
NX = 4
BLK = 128
VMEM_LIMIT = 16 * 1024 * 1024


def y_pairs(shift):
    return [(z * NY + y, z * NY + (y + shift) % NY) for z in range(NZ) for y in range(NY)]


def z_pairs(shift):
    return [(z * NY + y, (z + shift) % NZ * NY + y) for z in range(NZ) for y in range(NY)]


def x_pairs(shift):
    return [
        ((h * NX + x) * 2 + c, (h * NX + (x + shift) % NX) * 2 + c)
        for h in range(2)
        for x in range(NX)
        for c in range(2)
    ]


CORE_PAIRS = [(i, i ^ 1) for i in range(16)]
HALF_PAIRS = [(i, i ^ 8) for i in range(16)]


def block_grads(cols, half, pos_ref, chip_ref, acts_ref, up_ref, *outs):
    def column(c, carry):
        up = up_ref[:, pl.ds(pl.multiple_of(c * BLK, BLK), BLK)]
        for h, out in enumerate(outs):
            for k in range(half):
                slot = c * half + k
                block = acts_ref[pos_ref[h * cols * half + slot]]
                grad = lax.dot_general(
                    block, up, (((0,), (0,)), ((), ())), preferred_element_type=jnp.float32
                ).astype(jnp.bfloat16)
                for chip in range(8):
                    out[chip_ref[chip], slot] = grad[chip * 16 : (chip + 1) * 16]
        return carry

    lax.fori_loop(0, cols, column, 0)


def project(cols, half, pos_ref, chip_ref, acts_ref, up_ref, w0_ref, w1_ref, hidden_ref, *rest):
    parts, total = rest[:-1], rest[-1]
    total[...] = jnp.zeros_like(total)

    def column(c, carry):
        lanes = pl.ds(pl.multiple_of(c * BLK, BLK), BLK)
        up = up_ref[:, lanes]
        hidden = jnp.zeros((up.shape[0], BLK), jnp.float32)
        for h, w_ref in enumerate((w0_ref, w1_ref)):
            for k in range(0, half, 2):
                rows = []
                blocks = []
                weights = []
                for j in range(2):
                    slot = c * half + k + j
                    rows.append(pos_ref[h * cols * half + slot])
                    blocks.append(acts_ref[rows[-1]])
                    weights += [w_ref[chip_ref[chip], slot] for chip in range(8)]
                weight = jnp.concatenate(weights, axis=0)
                hidden += jnp.dot(
                    jnp.concatenate(blocks, axis=1), weight, preferred_element_type=jnp.float32
                )
                back = lax.dot_general(
                    up, weight, (((1,), (1,)), ((), ())), preferred_element_type=jnp.float32
                )
                for j in range(2):
                    total[rows[j]] += back[:, j * BLK : (j + 1) * BLK]
        hidden_ref[:, lanes] = hidden.astype(jnp.bfloat16)
        return carry

    lax.fori_loop(0, cols, column, 0)
    start = 0
    for part in parts:
        part[...] = total[start : start + part.shape[0]].astype(jnp.bfloat16)
        start += part.shape[0]


def kernel_call(body, outs, scratch, flops, ins):
    specs = [pl.BlockSpec(memory_space=pltpu.SMEM)] * 2
    specs += [pl.BlockSpec(memory_space=pltpu.VMEM)] * (len(ins) - 2)
    moved = sum(a.size * a.dtype.itemsize for a in list(ins) + list(outs))
    return pl.pallas_call(
        body,
        out_shape=outs,
        in_specs=specs,
        out_specs=[pl.BlockSpec(memory_space=pltpu.VMEM)] * len(outs),
        scratch_shapes=scratch,
        compiler_params=pltpu.CompilerParams(vmem_limit_bytes=VMEM_LIMIT),
        cost_estimate=pl.CostEstimate(flops=flops, bytes_accessed=moved, transcendentals=0),
    )(*ins)


def f32(a):
    return a.astype(jnp.float32)


def z_step(a, q):
    with jax.named_scope("z_lo"):
        return lax.ppermute(a, "mp", z_pairs(q))


def y_step(a, p):
    with jax.named_scope("y"):
        return lax.ppermute(a, "mp", y_pairs(p))


def x_step(a, s):
    with jax.named_scope("x"):
        return lax.ppermute(a, "dp", x_pairs(s))


def zh_step(a):
    with jax.named_scope("z_hi"):
        return lax.ppermute(a, "dp", HALF_PAIRS)


def core_step(a):
    with jax.named_scope("core"):
        return lax.ppermute(a, "dp", CORE_PAIRS)


def tie(values, *after):
    return lax.optimization_barrier((values, after))[0]


def gather_direct(step, a):
    return [a] + [step(a, s) for s in range(1, 4)]


def gather_passed(step, a):
    n = a.shape[0] // 2
    back, ahead = step(a, 1), step(a, -1)
    opposite = jnp.concatenate([step(back[:n], 1), step(ahead[n:], -1)])
    return [a, back, opposite, ahead]


def sum_direct(step, p0, p1, p2a, p2b, p3):
    return f32(p0) + f32(step(p1, -1)) + f32(step(jnp.concatenate([p2a, p2b]), -2)) + f32(step(p3, -3))


def sum_passed(step, p0, p1, p2a, p2b, p3):
    n = p2a.shape[0]
    ahead, back = step(p2a, 1), step(p2b, -1)
    p3 = jnp.concatenate([(f32(p3[:n]) + f32(ahead)).astype(p3.dtype), p3[n:]])
    p1 = jnp.concatenate([p1[:n], (f32(p1[n:]) + f32(back)).astype(p1.dtype)])
    return f32(p0) + f32(step(p3, 1)) + f32(step(p1, -1))


def shards(acts, grad_out, values, block_rows, block_count):
    tokens = acts.shape[0]
    cols, slots = block_rows.shape
    half = slots // 2
    own_blocks = acts.shape[1] // BLK
    bf = jnp.bfloat16
    dp, mp = lax.axis_index("dp"), lax.axis_index("mp")
    core, x, zh = dp % 2, dp // 2 % NX, dp // (2 * NX)
    z, y = mp // NY, mp % NY
    first = core == 0

    def halves(a):
        return (
            jnp.where(first, a[:, :half], a[:, half:]),
            jnp.where(first, a[:, half:], a[:, :half]),
        )

    def ordered(mine, other, axis):
        return jnp.where(
            first,
            jnp.concatenate([mine, other], axis=axis),
            jnp.concatenate([other, mine], axis=axis),
        )

    blocks = NZ * NY * own_blocks
    live = jnp.arange(slots, dtype=jnp.int32)[None, :] < block_count[:, None]
    owner = block_rows // own_blocks
    place = ((y - owner % NY) % NY * NZ + (z - owner // NY) % NZ) * own_blocks + block_rows % own_blocks
    place = jnp.where(live, place, blocks)
    pos = jnp.concatenate([a.reshape(-1) for a in halves(place)])
    chips = jnp.arange(8, dtype=jnp.int32)
    chip = (zh + chips // NX) % 2 * NX + (x - chips % NX) % NX

    mine, other = halves(values)
    rows16 = ordered(mine, core_step(other), 2).reshape(cols * half, 16, BLK)

    own = acts.reshape(tokens, own_blocks, BLK).transpose(1, 0, 2)
    along_z = jnp.concatenate([own] + [z_step(own, q) for q in range(1, NZ)])
    far16 = zh_step(rows16)
    near1, near3 = x_step(rows16, 1), x_step(rows16, 3)
    along_z = tie(along_z, rows16)
    whole = gather_passed(y_step, along_z)
    n = rows16.shape[0] // 2
    near = [rows16, near1, jnp.concatenate([x_step(near1[:n], 1), x_step(near3[n:], -1)]), near3]
    far = gather_direct(x_step, far16)
    whole = jnp.concatenate(whole + [jnp.zeros((1, tokens, BLK), bf)])
    w8 = jnp.stack(near + far)
    w8_other = core_step(w8)

    flops = 2 * tokens * BLK * BLK * cols * slots
    shape = jax.ShapeDtypeStruct((8, cols * half, 16, BLK), bf)
    mine, other = kernel_call(
        functools.partial(block_grads, cols, half),
        [shape, shape],
        [],
        flops,
        (pos, chip, whole, grad_out),
    )
    came = core_step(other)

    part = jax.ShapeDtypeStruct((NZ * own_blocks, tokens, BLK), bf)
    half_part = jax.ShapeDtypeStruct((NZ * own_blocks // 2, tokens, BLK), bf)
    hidden_out, *parts = kernel_call(
        functools.partial(project, cols, half),
        [jax.ShapeDtypeStruct(grad_out.shape, bf), part, part, half_part, half_part, part],
        [pltpu.VMEM((blocks + 1, tokens, BLK), jnp.float32)],
        2 * flops,
        (pos, chip, whole, grad_out, w8, w8_other),
    )

    def over_x(zr, after=None):
        sums = [(f32(mine[zr * NX + s]) + f32(came[zr * NX + s])).astype(bf) for s in range(NX)]
        if after is not None:
            sums = tie(sums, after)
        n = sums[2].shape[0] // 2
        return sum_passed(x_step, sums[0], sums[1], sums[2][:n], sums[2][n:], sums[3])

    away = over_x(1).astype(bf)
    total = over_x(0, away)
    away = zh_step(away)
    total = (total + f32(away)).reshape(cols, half, 16, BLK)
    keep = jnp.where(first, total[:, :, :8], total[:, :, 8:])
    send = jnp.where(first, total[:, :, 8:], total[:, :, :8])
    grad_values = ordered(keep, core_step(send), 1)

    rest = sum_passed(y_step, *parts)
    total = rest[:own_blocks]
    for q in range(1, NZ):
        total += f32(z_step(rest[q * own_blocks : (q + 1) * own_blocks].astype(bf), -q))
    grad_acts = total.transpose(1, 0, 2).reshape(tokens, own_blocks * BLK).astype(bf)
    return hidden_out, grad_acts, grad_values


def solution(mesh):
    placed = (P("dp", "mp"), P("dp", "mp"), P("mp", None, "dp", None), P("mp", None), P("mp"))
    return jax.shard_map(
        shards,
        mesh=mesh,
        in_specs=placed,
        out_specs=(P("dp", "mp"), P("dp", "mp"), P("mp", None, "dp", None)),
        check_vma=False,
    )
```

```python
import functools

import jax
import jax.numpy as jnp
from jax import lax
from jax.experimental import pallas as pl
from jax.experimental.pallas import tpu as pltpu
from jax.sharding import PartitionSpec as P

NZ = 4
NY = 4
NX = 4
BLK = 128
VMEM_LIMIT = 16 * 1024 * 1024


def y_pairs(shift):
    return [(z * NY + y, z * NY + (y + shift) % NY) for z in range(NZ) for y in range(NY)]


def z_pairs(shift):
    return [(z * NY + y, (z + shift) % NZ * NY + y) for z in range(NZ) for y in range(NY)]


def x_pairs(shift):
    return [
        ((h * NX + x) * 2 + c, (h * NX + (x + shift) % NX) * 2 + c)
        for h in range(2)
        for x in range(NX)
        for c in range(2)
    ]


CORE_PAIRS = [(i, i ^ 1) for i in range(16)]
HALF_PAIRS = [(i, i ^ 8) for i in range(16)]


def block_grads(cols, half, pos_ref, chip_ref, acts_ref, up_ref, *outs):
    def column(c, carry):
        up = up_ref[:, pl.ds(pl.multiple_of(c * BLK, BLK), BLK)]
        for h, out in enumerate(outs):
            for k in range(half):
                slot = c * half + k
                block = acts_ref[pos_ref[h * cols * half + slot]]
                grad = lax.dot_general(
                    block, up, (((0,), (0,)), ((), ())), preferred_element_type=jnp.float32
                ).astype(jnp.bfloat16)
                for chip in range(8):
                    out[chip_ref[chip], slot] = grad[chip * 16 : (chip + 1) * 16]
        return carry

    lax.fori_loop(0, cols, column, 0)


def pair(half, cols, c, h, k, pos_ref, chip_ref, w_ref):
    slots = [c * half + k, c * half + k + 1]
    rows = [pos_ref[h * cols * half + slot] for slot in slots]
    weight = jnp.concatenate([w_ref[chip_ref[chip], slot] for slot in slots for chip in range(8)], axis=0)
    return rows, weight


def project_back(cols, half, pos_ref, chip_ref, up_ref, w0_ref, w1_ref, *rest):
    parts, total = rest[:-1], rest[-1]
    total[...] = jnp.zeros_like(total)

    def column(c, carry):
        up = up_ref[:, pl.ds(pl.multiple_of(c * BLK, BLK), BLK)]
        for h, w_ref in enumerate((w0_ref, w1_ref)):
            for k in range(0, half, 2):
                rows, weight = pair(half, cols, c, h, k, pos_ref, chip_ref, w_ref)
                back = lax.dot_general(
                    up, weight, (((1,), (1,)), ((), ())), preferred_element_type=jnp.float32
                )
                for j in range(2):
                    total[rows[j]] += back[:, j * BLK : (j + 1) * BLK]
        return carry

    lax.fori_loop(0, cols, column, 0)
    start = 0
    for part in parts:
        for piece in range(part.shape[0]):
            for lane in range(0, part.shape[2], BLK):
                part[piece, :, lane : lane + BLK] = total[start].astype(jnp.bfloat16)
                start += 1


def project(cols, half, pos_ref, chip_ref, acts_ref, w0_ref, w1_ref, hidden_ref):
    def column(c, carry):
        hidden = jnp.zeros((acts_ref.shape[1], BLK), jnp.float32)
        for h, w_ref in enumerate((w0_ref, w1_ref)):
            for k in range(0, half, 2):
                rows, weight = pair(half, cols, c, h, k, pos_ref, chip_ref, w_ref)
                blocks = jnp.concatenate([acts_ref[row] for row in rows], axis=1)
                hidden += jnp.dot(blocks, weight, preferred_element_type=jnp.float32)
        hidden_ref[:, pl.ds(pl.multiple_of(c * BLK, BLK), BLK)] = hidden.astype(jnp.bfloat16)
        return carry

    lax.fori_loop(0, cols, column, 0)


def kernel_call(body, outs, scratch, flops, ins):
    specs = [pl.BlockSpec(memory_space=pltpu.SMEM)] * 2
    specs += [pl.BlockSpec(memory_space=pltpu.VMEM)] * (len(ins) - 2)
    moved = sum(a.size * a.dtype.itemsize for a in list(ins) + list(outs))
    return pl.pallas_call(
        body,
        out_shape=outs,
        in_specs=specs,
        out_specs=[pl.BlockSpec(memory_space=pltpu.VMEM)] * len(outs),
        scratch_shapes=scratch,
        compiler_params=pltpu.CompilerParams(vmem_limit_bytes=VMEM_LIMIT),
        cost_estimate=pl.CostEstimate(flops=flops, bytes_accessed=moved, transcendentals=0),
    )(*ins)


def f32(a):
    return a.astype(jnp.float32)


def z_step(a, q):
    with jax.named_scope("z_lo"):
        return lax.ppermute(a, "mp", z_pairs(q))


def y_step(a, p):
    with jax.named_scope("y"):
        return lax.ppermute(a, "mp", y_pairs(p))


def x_step(a, s):
    with jax.named_scope("x"):
        return lax.ppermute(a, "dp", x_pairs(s))


def zh_step(a):
    with jax.named_scope("z_hi"):
        return lax.ppermute(a, "dp", HALF_PAIRS)


def core_step(a):
    with jax.named_scope("core"):
        return lax.ppermute(a, "dp", CORE_PAIRS)


def tie(values, *after):
    return lax.optimization_barrier((values, after))[0]


def gather_direct(step, a):
    return [a] + [step(a, s) for s in range(1, 4)]


def gather_passed(step, a):
    n = a.shape[0] // 2
    back, ahead = step(a, 1), step(a, -1)
    opposite = jnp.concatenate([step(back[:n], 1), step(ahead[n:], -1)])
    return [a, back, opposite, ahead]


def sum_direct(step, p0, p1, p2a, p2b, p3):
    return f32(p0) + f32(step(p1, -1)) + f32(step(jnp.concatenate([p2a, p2b]), -2)) + f32(step(p3, -3))


def sum_passed(step, p0, p1, p2a, p2b, p3):
    n = p2a.shape[0]
    ahead, back = step(p2a, 1), step(p2b, -1)
    p3 = jnp.concatenate([(f32(p3[:n]) + f32(ahead)).astype(p3.dtype), p3[n:]])
    p1 = jnp.concatenate([p1[:n], (f32(p1[n:]) + f32(back)).astype(p1.dtype)])
    return f32(p0) + f32(step(p3, 1)) + f32(step(p1, -1))


def shards(acts, grad_out, values, block_rows, block_count):
    tokens = acts.shape[0]
    cols, slots = block_rows.shape
    half = slots // 2
    own_blocks = acts.shape[1] // BLK
    bf = jnp.bfloat16
    dp, mp = lax.axis_index("dp"), lax.axis_index("mp")
    core, x, zh = dp % 2, dp // 2 % NX, dp // (2 * NX)
    z, y = mp // NY, mp % NY
    first = core == 0

    def halves(a):
        return (
            jnp.where(first, a[:, :half], a[:, half:]),
            jnp.where(first, a[:, half:], a[:, :half]),
        )

    def ordered(mine, other, axis):
        return jnp.where(
            first,
            jnp.concatenate([mine, other], axis=axis),
            jnp.concatenate([other, mine], axis=axis),
        )

    blocks = NZ * NY * own_blocks
    live = jnp.arange(slots, dtype=jnp.int32)[None, :] < block_count[:, None]
    owner = block_rows // own_blocks
    place = ((y - owner % NY) % NY * NZ + (z - owner // NY) % NZ) * own_blocks + block_rows % own_blocks
    place = jnp.where(live, place, blocks)
    pos = jnp.concatenate([a.reshape(-1) for a in halves(place)])
    chips = jnp.arange(8, dtype=jnp.int32)
    chip = (zh + chips // NX) % 2 * NX + (x - chips % NX) % NX

    mine, other = halves(values)
    rows16 = ordered(mine, core_step(other), 2).reshape(cols * half, 16, BLK)

    own = acts.reshape(tokens, own_blocks, BLK).transpose(1, 0, 2)
    along_z = jnp.concatenate([own] + [z_step(own, q) for q in range(1, NZ)])
    far16 = zh_step(rows16)
    near1, near3 = x_step(rows16, 1), x_step(rows16, 3)
    along_z = tie(along_z, rows16)
    whole = gather_passed(y_step, along_z)
    n = rows16.shape[0] // 2
    near = [rows16, near1, jnp.concatenate([x_step(near1[:n], 1), x_step(near3[n:], -1)]), near3]
    far = gather_direct(x_step, far16)
    whole = jnp.concatenate(whole + [jnp.zeros((1, tokens, BLK), bf)])
    w8 = jnp.stack(near + far)
    w8_other = core_step(w8)

    flops = 2 * tokens * BLK * BLK * cols * slots
    shape = jax.ShapeDtypeStruct((8, cols * half, 16, BLK), bf)
    mine, other = kernel_call(
        functools.partial(block_grads, cols, half),
        [shape, shape],
        [],
        flops,
        (pos, chip, whole, grad_out),
    )
    came = core_step(other)

    part = jax.ShapeDtypeStruct((NZ, *acts.shape), bf)
    half_part = jax.ShapeDtypeStruct((NZ // 2, *acts.shape), bf)
    parts = kernel_call(
        functools.partial(project_back, cols, half),
        [part, part, half_part, half_part, part],
        [pltpu.VMEM((blocks + 1, tokens, BLK), jnp.float32)],
        flops,
        (pos, chip, grad_out, w8, w8_other),
    )

    def over_x(zr, after=None):
        sums = [(f32(mine[zr * NX + s]) + f32(came[zr * NX + s])).astype(bf) for s in range(NX)]
        if after is not None:
            sums = tie(sums, after)
        n = sums[2].shape[0] // 2
        return sum_passed(x_step, sums[0], sums[1], sums[2][:n], sums[2][n:], sums[3])

    away = over_x(1).astype(bf)
    total = over_x(0, away)
    away = zh_step(away)
    total = (total + f32(away)).reshape(cols, half, 16, BLK)
    keep = jnp.where(first, total[:, :, :8], total[:, :, 8:])
    send = jnp.where(first, total[:, :, 8:], total[:, :, :8])
    grad_values = ordered(keep, core_step(send), 1)

    rest = sum_passed(y_step, *parts)
    (hidden_out,) = kernel_call(
        functools.partial(project, cols, half),
        [jax.ShapeDtypeStruct(grad_out.shape, bf)],
        [],
        flops,
        (pos, chip, tie(whole, away), w8, w8_other),
    )
    total = tie(rest[0], hidden_out)
    for q in range(1, NZ):
        total += f32(z_step(rest[q].astype(bf), -q))
    grad_acts = total.astype(bf)
    return hidden_out, grad_acts, grad_values


def solution(mesh):
    placed = (P("dp", "mp"), P("dp", "mp"), P("mp", None, "dp", None), P("mp", None), P("mp"))
    return jax.shard_map(
        shards,
        mesh=mesh,
        in_specs=placed,
        out_specs=(P("dp", "mp"), P("dp", "mp"), P("mp", None, "dp", None)),
        check_vma=False,
    )
```

```python
import functools

import jax
import jax.numpy as jnp
from jax import lax
from jax.experimental import pallas as pl
from jax.experimental.pallas import tpu as pltpu
from jax.sharding import PartitionSpec as P

NZ = 4
NY = 4
NX = 4
BLK = 128
VMEM_LIMIT = 16 * 1024 * 1024


def y_pairs(shift):
    return [(z * NY + y, z * NY + (y + shift) % NY) for z in range(NZ) for y in range(NY)]


def z_pairs(shift):
    return [(z * NY + y, (z + shift) % NZ * NY + y) for z in range(NZ) for y in range(NY)]


def x_pairs(shift):
    return [
        ((h * NX + x) * 2 + c, (h * NX + (x + shift) % NX) * 2 + c)
        for h in range(2)
        for x in range(NX)
        for c in range(2)
    ]


CORE_PAIRS = [(i, i ^ 1) for i in range(16)]
HALF_PAIRS = [(i, i ^ 8) for i in range(16)]


def block_grads(cols, half, pos_ref, chip_ref, acts_ref, up_ref, *outs):
    def column(c, carry):
        up = up_ref[:, pl.ds(pl.multiple_of(c * BLK, BLK), BLK)]
        for h, out in enumerate(outs):
            for k in range(half):
                slot = c * half + k
                block = acts_ref[pos_ref[h * cols * half + slot]]
                grad = lax.dot_general(
                    block, up, (((0,), (0,)), ((), ())), preferred_element_type=jnp.float32
                ).astype(jnp.bfloat16)
                for chip in range(8):
                    out[chip_ref[chip], slot] = grad[chip * 16 : (chip + 1) * 16]
        return carry

    lax.fori_loop(0, cols, column, 0)


def pair(half, cols, c, h, k, pos_ref, chip_ref, w_ref):
    slots = [c * half + k, c * half + k + 1]
    rows = [pos_ref[h * cols * half + slot] for slot in slots]
    weight = jnp.concatenate([w_ref[chip_ref[chip], slot] for slot in slots for chip in range(8)], axis=0)
    return rows, weight


def project_back(cols, half, pos_ref, chip_ref, up_ref, w0_ref, w1_ref, *rest):
    parts, total = rest[:-1], rest[-1]
    total[...] = jnp.zeros_like(total)

    def column(c, carry):
        up = up_ref[:, pl.ds(pl.multiple_of(c * BLK, BLK), BLK)]
        for h, w_ref in enumerate((w0_ref, w1_ref)):
            for k in range(0, half, 2):
                rows, weight = pair(half, cols, c, h, k, pos_ref, chip_ref, w_ref)
                back = lax.dot_general(
                    up, weight, (((1,), (1,)), ((), ())), preferred_element_type=jnp.float32
                )
                for j in range(2):
                    total[rows[j]] += back[:, j * BLK : (j + 1) * BLK]
        return carry

    lax.fori_loop(0, cols, column, 0)
    start = 0
    for part in parts:
        for piece in range(part.shape[0]):
            for lane in range(0, part.shape[2], BLK):
                part[piece, :, lane : lane + BLK] = total[start].astype(jnp.bfloat16)
                start += 1


def project(cols, half, pos_ref, chip_ref, acts_ref, w0_ref, w1_ref, hidden_ref):
    def column(c, carry):
        hidden = jnp.zeros((acts_ref.shape[1], BLK), jnp.float32)
        for h, w_ref in enumerate((w0_ref, w1_ref)):
            for k in range(0, half, 2):
                rows, weight = pair(half, cols, c, h, k, pos_ref, chip_ref, w_ref)
                blocks = jnp.concatenate([acts_ref[row] for row in rows], axis=1)
                hidden += jnp.dot(blocks, weight, preferred_element_type=jnp.float32)
        hidden_ref[:, pl.ds(pl.multiple_of(c * BLK, BLK), BLK)] = hidden.astype(jnp.bfloat16)
        return carry

    lax.fori_loop(0, cols, column, 0)


def kernel_call(body, outs, scratch, flops, ins):
    specs = [pl.BlockSpec(memory_space=pltpu.SMEM)] * 2
    specs += [pl.BlockSpec(memory_space=pltpu.VMEM)] * (len(ins) - 2)
    moved = sum(a.size * a.dtype.itemsize for a in list(ins) + list(outs))
    return pl.pallas_call(
        body,
        out_shape=outs,
        in_specs=specs,
        out_specs=[pl.BlockSpec(memory_space=pltpu.VMEM)] * len(outs),
        scratch_shapes=scratch,
        compiler_params=pltpu.CompilerParams(vmem_limit_bytes=VMEM_LIMIT),
        cost_estimate=pl.CostEstimate(flops=flops, bytes_accessed=moved, transcendentals=0),
    )(*ins)


def f32(a):
    return a.astype(jnp.float32)


def z_step(a, q):
    with jax.named_scope("z_lo"):
        return lax.ppermute(a, "mp", z_pairs(q))


def y_step(a, p):
    with jax.named_scope("y"):
        return lax.ppermute(a, "mp", y_pairs(p))


def x_step(a, s):
    with jax.named_scope("x"):
        return lax.ppermute(a, "dp", x_pairs(s))


def zh_step(a):
    with jax.named_scope("z_hi"):
        return lax.ppermute(a, "dp", HALF_PAIRS)


def core_step(a):
    with jax.named_scope("core"):
        return lax.ppermute(a, "dp", CORE_PAIRS)


def tie(values, *after):
    return lax.optimization_barrier((values, after))[0]


def gather_direct(step, a):
    return [a] + [step(a, s) for s in range(1, 4)]


def gather_passed(step, a):
    n = a.shape[0] // 2
    back, ahead = step(a, 1), step(a, -1)
    opposite = jnp.concatenate([step(back[:n], 1), step(ahead[n:], -1)])
    return [a, back, opposite, ahead]


def sum_direct(step, p0, p1, p2a, p2b, p3):
    return f32(p0) + f32(step(p1, -1)) + f32(step(jnp.concatenate([p2a, p2b]), -2)) + f32(step(p3, -3))


def sum_passed(step, p0, p1, p2a, p2b, p3):
    n = p2a.shape[0]
    ahead, back = step(p2a, 1), step(p2b, -1)
    p3 = jnp.concatenate([(f32(p3[:n]) + f32(ahead)).astype(p3.dtype), p3[n:]])
    p1 = jnp.concatenate([p1[:n], (f32(p1[n:]) + f32(back)).astype(p1.dtype)])
    return f32(p0) + f32(step(p3, 1)) + f32(step(p1, -1))


def shards(acts, grad_out, values, block_rows, block_count):
    tokens = acts.shape[0]
    cols, slots = block_rows.shape
    half = slots // 2
    own_blocks = acts.shape[1] // BLK
    bf = jnp.bfloat16
    dp, mp = lax.axis_index("dp"), lax.axis_index("mp")
    core, x, zh = dp % 2, dp // 2 % NX, dp // (2 * NX)
    z, y = mp // NY, mp % NY
    first = core == 0

    def halves(a):
        return (
            jnp.where(first, a[:, :half], a[:, half:]),
            jnp.where(first, a[:, half:], a[:, :half]),
        )

    def ordered(mine, other, axis):
        return jnp.where(
            first,
            jnp.concatenate([mine, other], axis=axis),
            jnp.concatenate([other, mine], axis=axis),
        )

    blocks = NZ * NY * own_blocks
    live = jnp.arange(slots, dtype=jnp.int32)[None, :] < block_count[:, None]
    owner = block_rows // own_blocks
    place = ((y - owner % NY) % NY * NZ + (z - owner // NY) % NZ) * own_blocks + block_rows % own_blocks
    place = jnp.where(live, place, blocks)
    pos = jnp.concatenate([a.reshape(-1) for a in halves(place)])
    chips = jnp.arange(8, dtype=jnp.int32)
    chip = (zh + chips // NX) % 2 * NX + (x - chips % NX) % NX

    came = core_step(values)
    rows16 = jnp.where(
        first,
        jnp.concatenate([values[:, :half], came[:, :half]], axis=2),
        jnp.concatenate([came[:, half:], values[:, half:]], axis=2),
    ).reshape(cols * half, 16, BLK)

    own = acts.reshape(tokens, own_blocks, BLK).transpose(1, 0, 2)
    along_z = jnp.concatenate([own] + [z_step(own, q) for q in range(1, NZ)])
    far16 = zh_step(rows16)
    near1, near3 = x_step(rows16, 1), x_step(rows16, 3)
    along_z = tie(along_z, rows16)
    whole = gather_passed(y_step, along_z)
    n = rows16.shape[0] // 2
    near = [rows16, near1, jnp.concatenate([x_step(near1[:n], 1), x_step(near3[n:], -1)]), near3]
    far = gather_direct(x_step, far16)
    whole = jnp.concatenate(whole + [jnp.zeros((1, tokens, BLK), bf)])
    w8 = jnp.stack(near + far)
    w8_other = core_step(w8)

    flops = 2 * tokens * BLK * BLK * cols * slots
    shape = jax.ShapeDtypeStruct((8, cols * half, 16, BLK), bf)
    mine, other = kernel_call(
        functools.partial(block_grads, cols, half),
        [shape, shape],
        [],
        flops,
        (pos, chip, whole, grad_out),
    )
    came = core_step(other)

    part = jax.ShapeDtypeStruct((NZ, *acts.shape), bf)
    half_part = jax.ShapeDtypeStruct((NZ // 2, *acts.shape), bf)
    parts = kernel_call(
        functools.partial(project_back, cols, half),
        [part, part, half_part, half_part, part],
        [pltpu.VMEM((blocks + 1, tokens, BLK), jnp.float32)],
        flops,
        (pos, chip, grad_out, w8, w8_other),
    )

    def over_x(zr, after=None):
        sums = [(f32(mine[zr * NX + s]) + f32(came[zr * NX + s])).astype(bf) for s in range(NX)]
        if after is not None:
            sums = tie(sums, after)
        n = sums[2].shape[0] // 2
        return sum_passed(x_step, sums[0], sums[1], sums[2][:n], sums[2][n:], sums[3])

    away = over_x(1).astype(bf)
    total = over_x(0, away)
    away = zh_step(away)
    total = (total + f32(away)).reshape(cols, half, 16, BLK)
    keep = jnp.where(first, total[:, :, :8], total[:, :, 8:])
    send = jnp.where(first, total[:, :, 8:], total[:, :, :8])
    grad_values = ordered(keep, core_step(send), 1)

    rest = sum_passed(y_step, *parts)
    (hidden_out,) = kernel_call(
        functools.partial(project, cols, half),
        [jax.ShapeDtypeStruct(grad_out.shape, bf)],
        [],
        flops,
        (pos, chip, tie(whole, away), w8, w8_other),
    )
    total = tie(rest[0], hidden_out)
    for q in range(1, NZ):
        total += f32(z_step(rest[q].astype(bf), -q))
    grad_acts = total.astype(bf)
    return hidden_out, grad_acts, grad_values


def solution(mesh):
    placed = (P("dp", "mp"), P("dp", "mp"), P("mp", None, "dp", None), P("mp", None), P("mp"))
    return jax.shard_map(
        shards,
        mesh=mesh,
        in_specs=placed,
        out_specs=(P("dp", "mp"), P("dp", "mp"), P("mp", None, "dp", None)),
        check_vma=False,
    )
```
